512 devices in a mesh: dp: 8 (over x, core), fsdp: 64 (over z, y).
Axes of the slice: x: 4, y: 4, z: 16, core: 2. Of those that a mesh axis runs over, the one named last changes fastest.
Arguments:
- grad_parts: bfloat16 [8, 4096, 16384], P('dp', 'fsdp'), may hold values from -6 to 6
- slot_table: int32 [8, 32], P('dp'), may hold values from 0 to 31, each once within a row
- left_stat: bfloat16 [8, 32, 512, 512], P('dp', None, 'fsdp'), may hold values from -6 to 6
- right_stat: bfloat16 [8, 32, 512, 512], P('dp', None, 'fsdp'), may hold values from -6 to 6
- left_root: bfloat16 [8, 32, 512, 512], P('dp', None, 'fsdp'), may hold values from -0.25 to 0.25
- right_root: bfloat16 [8, 32, 512, 512], P('dp', None, 'fsdp'), may hold values from -0.25 to 0.25
Outputs:
- left_new: bfloat16 [8, 32, 512, 512], P('dp', None, 'fsdp')
- right_new: bfloat16 [8, 32, 512, 512], P('dp', None, 'fsdp')
- update: bfloat16 [4096, 16384], P('fsdp', 'dp')
The draws below stay inside these ranges and needn't reach their ends.
Inputs may be any that keep to these rules, and one draw needn't show every extreme that they name: Each row of slot_table is a permutation: slot_table[d, k] is where block k of band d keeps its factors.
All inputs are finite; a program needn't handle non-finite values.
Results may differ from the reference program's by a relative error of at most 0.022.
Values may be sent and summed in bfloat16 or wider, within the bound.
No kernel may reach another device: no remote copies, remote signals or barrier semaphores. Data moves between devices by JAX's collectives and lax.ppermute only.
A program may use at most 64 MiB of HBM per device.

```python
import jax
import jax.numpy as jnp
from jax import lax

ROWS = 4096
COLS = 16384
BLOCK = 512
NB = 32
N_DP = 8
N_FSDP = 64


def block_scale(rng, extent, cuts, low, top_value):
    def one(dim, parts):
        steps = jax.random.uniform(jax.random.fold_in(jax.random.fold_in(rng, 6), dim), (parts,), jnp.float32, low / len(cuts), top_value / len(cuts))
        return jnp.repeat(jnp.exp(steps), extent[dim] // parts).reshape((-1,) + (1,) * (len(extent) - dim - 1))

    level = one(*cuts[0])
    for cut in cuts[1:]:
        level = level * one(*cut)
    return level


def centred(key, extent, spread, most, cuts=(), kind=jnp.bfloat16):
    values = spread * jax.random.normal(key, extent, jnp.float32)
    if cuts:
        values = values * block_scale(key, extent, cuts, -0.22, 0.18)
    return jnp.clip(values, -most, most).astype(kind)


def setup_inputs(seed: int = 0) -> dict:
    streams_of = jax.random.split(jax.random.key(seed), 7)
    return {
        "grad_parts": centred(streams_of[0], (N_DP, ROWS, COLS), 1.0, 6.0, ((0, 8), (1, 64))),
        "slot_table": jax.vmap(lambda own: jax.random.permutation(own, NB))(jax.random.split(streams_of[1], N_DP)).reshape((N_DP, NB)).astype(jnp.int32),
        "left_stat": centred(streams_of[2], (N_DP, NB, BLOCK, BLOCK), 1.0, 6.0, ((0, 8), (2, 64))),
        "right_stat": centred(streams_of[3], (N_DP, NB, BLOCK, BLOCK), 1.0, 6.0, ((0, 8), (2, 64))),
        "left_root": centred(streams_of[4], (N_DP, NB, BLOCK, BLOCK), BLOCK ** -0.5, 0.25, ((0, 8), (2, 64))),
        "right_root": centred(streams_of[5], (N_DP, NB, BLOCK, BLOCK), BLOCK ** -0.5, 0.25, ((0, 8), (2, 64))),
    }


decay = 0.9


def to_blocks(matrix):
    nrb = ROWS // BLOCK
    ncb = COLS // (N_DP * BLOCK)
    piece = BLOCK // N_FSDP
    grid = matrix.reshape(N_FSDP, nrb, piece, N_DP, ncb, BLOCK)
    grid = grid.transpose(3, 1, 4, 0, 2, 5)
    return grid.reshape(N_DP, nrb * ncb, BLOCK, BLOCK)


def from_blocks(blocks):
    nrb = ROWS // BLOCK
    ncb = COLS // (N_DP * BLOCK)
    piece = BLOCK // N_FSDP
    grid = blocks.reshape(N_DP, nrb, ncb, N_FSDP, piece, BLOCK)
    grid = grid.transpose(3, 1, 4, 0, 2, 5)
    return grid.reshape(ROWS, COLS)


def one_band(inputs):
    blocks, table, lstat, rstat, lroot, rroot = inputs
    grads = blocks.astype(jnp.float32)
    left_gram = jnp.einsum("kij,klj->kil", grads, grads)
    right_gram = jnp.einsum("kji,kjl->kil", grads, grads)
    new_left = (decay * lstat[table].astype(jnp.float32) + (1.0 - decay) / BLOCK * left_gram).astype(jnp.bfloat16)
    new_right = (decay * rstat[table].astype(jnp.float32) + (1.0 - decay) / BLOCK * right_gram).astype(jnp.bfloat16)
    half = jnp.einsum("kij,kjl->kil", lroot[table].astype(jnp.float32), grads).astype(jnp.bfloat16)
    result = jnp.einsum("kij,kjl->kil", half.astype(jnp.float32), rroot[table].astype(jnp.float32)).astype(jnp.bfloat16)
    left_out = jnp.zeros_like(lstat).at[table].set(new_left)
    right_out = jnp.zeros_like(rstat).at[table].set(new_right)
    return left_out, right_out, result


def reference(grad_parts, slot_table, left_stat, right_stat, left_root, right_root):
    total = jnp.sum(grad_parts.astype(jnp.float32), axis=0).astype(jnp.bfloat16)
    blocks = to_blocks(total)
    left_new, right_new, updated = lax.map(one_band, (blocks, slot_table, left_stat, right_stat, left_root, right_root))
    return left_new, right_new, from_blocks(updated)
```

```python
import jax
import jax.numpy as jnp
from jax import lax
from jax.sharding import Mesh, PartitionSpec as P

decay = 0.9
bf16 = jnp.bfloat16
f32 = jnp.float32


def shift(value, axis, by):
    n = lax.axis_size(axis)
    return lax.ppermute(value, axis, [(i, (i + by) % n) for i in range(n)])


def gather_y(value):
    n = lax.axis_size("y")
    me = lax.axis_index("y")
    parts = [value] + [shift(value, "y", by) for by in range(1, n)]
    return jnp.stack([
        lax.select_n((me - owner) % n, *parts) for owner in range(n)
    ])


def sum_dp(grad):
    nx = lax.axis_size("x")
    core = lax.axis_index("core")
    x = lax.axis_index("x")
    rows = grad.shape[0]
    parts = grad.reshape(rows, nx, 2, -1)
    mine = lax.dynamic_index_in_dim(parts, core, 2, keepdims=False)
    other = lax.dynamic_index_in_dim(parts, 1 - core, 2, keepdims=False)
    got = lax.ppermute(other, "core", [(0, 1), (1, 0)])
    pair = (mine.astype(f32) + got.astype(f32)).astype(bf16)
    total = lax.dynamic_index_in_dim(pair, x, 1, keepdims=False).astype(f32)
    for by in range(1, nx):
        piece = lax.dynamic_index_in_dim(pair, (x + by) % nx, 1, keepdims=False)
        total = total + shift(piece, "x", by).astype(f32)
    return total.astype(bf16)


def local(grad_parts, slot_table, left_stat, right_stat, left_root, right_root):
    nz, ny = lax.axis_size("z"), lax.axis_size("y")
    y = lax.axis_index("y")
    nblocks, piece, block = left_stat.shape[1:]
    rows_dev = grad_parts.shape[1]
    nrb = rows_dev // piece
    ncb = nblocks // nrb
    per = nblocks // nz
    table = slot_table[0]

    roots = jnp.stack(
        [left_root[0].reshape(nz, per, piece, block), right_root[0].reshape(nz, per, piece, block)], 1
    )
    roots = lax.all_to_all(roots, "z", 0, 0, tiled=True)

    total = sum_dp(grad_parts[0])
    total = total.reshape(nrb, piece, ncb, block).transpose(0, 2, 1, 3).reshape(nblocks, piece, block)
    placed = jnp.zeros_like(total).at[table].set(total)
    grads = lax.all_to_all(placed.reshape(nz, per, piece, block), "z", 0, 0, tiled=True)

    def whole(parts):
        return gather_y(parts).transpose(2, 1, 0, 3, 4).reshape(per, block, block)

    def rows_of_y(value):
        picked = lax.dynamic_index_in_dim(value.reshape(per, nz, ny, piece, block), y, 2, keepdims=False)
        return picked.transpose(1, 0, 2, 3)

    right_full = whole(roots[:, 1])
    left_rows = roots[:, 0].transpose(1, 0, 2, 3).reshape(per, nz * piece, block)
    full = whole(grads)
    scale = (1.0 - decay) / block
    left_gram = (scale * jnp.einsum("mij,mkj->mik", full, full, preferred_element_type=f32)).astype(bf16)
    right_gram = (scale * jnp.einsum("mji,mjk->mik", full, full, preferred_element_type=f32)).astype(bf16)
    half = jnp.einsum("mij,mjk->mik", left_rows, full, preferred_element_type=f32).astype(bf16)
    result = jnp.einsum("mij,mjk->mik", half, right_full, preferred_element_type=f32).astype(bf16)
    result = result.reshape(per, nz, piece, block).transpose(1, 0, 2, 3)
    back = jnp.stack([rows_of_y(left_gram), rows_of_y(right_gram), result], 1)
    back = lax.all_to_all(back, "z", 0, 0, tiled=True)

    def settle(stat, gram):
        return (decay * stat.astype(f32) + gram.reshape(stat.shape).astype(f32)).astype(bf16)

    left_new = settle(left_stat, back[:, 0])
    right_new = settle(right_stat, back[:, 1])
    home = jnp.take(back[:, 2].reshape(nblocks, piece, block), table, axis=0)
    home = home.reshape(nrb, ncb, piece, block).transpose(0, 2, 1, 3)
    return left_new, right_new, home.reshape(rows_dev, ncb * block)


def solution(mesh):
    ny = 4
    devices = mesh.devices
    split = Mesh(
        devices.reshape(devices.shape[0] // 2, 2, devices.shape[1] // ny, ny), ("x", "core", "z", "y")
    )
    dp, fsdp = ("x", "core"), ("z", "y")
    factor = P(dp, None, fsdp, None)
    return jax.shard_map(
        local,
        mesh=split,
        in_specs=(P(dp, fsdp, None), P(dp, None), factor, factor, factor, factor),
        out_specs=(factor, factor, P(fsdp, dp)),
        check_vma=False,
    )
```

```python
import jax
import jax.numpy as jnp
from jax import lax
from jax.experimental import pallas as pl
from jax.experimental.pallas import tpu as pltpu
from jax.sharding import Mesh, PartitionSpec as P

decay = 0.9
bf16 = jnp.bfloat16
f32 = jnp.float32
params = pltpu.CompilerParams(vmem_limit_bytes=32 * 1024 * 1024)
wide = pltpu.CompilerParams(vmem_limit_bytes=56 * 1024 * 1024)


def shift(value, axis, by):
    n = lax.axis_size(axis)
    return lax.ppermute(value, axis, [(i, (i + by) % n) for i in range(n)])


def take_kernel(where, grad, out):
    out[0] = grad[...]


def stack_kernel(left, right, out):
    out[:, 0] = left[...]
    out[:, 1] = right[...]


def add_kernel(where, grad, got, own, *outs):
    step = pl.program_id(0)
    total = grad[...].astype(f32) + got[0].astype(f32)
    for i, out in enumerate(outs):

        @pl.when(step == i)
        def _():
            out[...] = total.astype(bf16)

    @pl.when(step == len(outs))
    def _():
        own[...] = total


def total_kernel(table, own, first, second, third, out):
    nblocks, piece, block = out.shape
    ncb = own.shape[1] // block
    total = own[...] + first[...].astype(f32) + second[...].astype(f32) + third[...].astype(f32)
    for k in range(nblocks):
        row, col = k // ncb * piece, k % ncb * block
        out[table[k]] = total[row : row + piece, col : col + block].astype(bf16)


def spec(shape):
    return pl.BlockSpec(shape, lambda *_: (0,) * len(shape))


def stack_roots(left, right):
    nz, per, piece, block = left.shape
    half = nz // 2
    return pl.pallas_call(
        stack_kernel,
        grid=(2,),
        in_specs=[pl.BlockSpec((half, per, piece, block), lambda i: (i, 0, 0, 0))] * 2,
        out_specs=pl.BlockSpec((half, 2, per, piece, block), lambda i: (i, 0, 0, 0, 0)),
        out_shape=jax.ShapeDtypeStruct((nz, 2, per, piece, block), bf16),
        cost_estimate=pl.CostEstimate(flops=0, bytes_accessed=8 * left.size, transcendentals=0),
        compiler_params=params,
        name="stack_roots",
    )(left, right)


def sum_dp(grad, table, nblocks, piece, block):
    nx = lax.axis_size("x")
    core = lax.axis_index("core")
    x = lax.axis_index("x")
    rows, cols = grad.shape
    band = cols // (2 * nx)
    other = pl.pallas_call(
        take_kernel,
        grid_spec=pltpu.PrefetchScalarGridSpec(
            num_scalar_prefetch=1,
            grid=(nx,),
            in_specs=[pl.BlockSpec((rows, band), lambda i, s: (0, 2 * i + s[0]))],
            out_specs=pl.BlockSpec((1, rows, band), lambda i, s: (i, 0, 0)),
        ),
        out_shape=jax.ShapeDtypeStruct((nx, rows, band), bf16),
        cost_estimate=pl.CostEstimate(flops=0, bytes_accessed=2 * rows * cols, transcendentals=0),
        compiler_params=params,
        name="other_core_bands",
    )((1 - core).astype(jnp.int32).reshape(1), grad)
    got = lax.ppermute(other, "core", [(0, 1), (1, 0)])

    order = (2, 1, 3, 0)
    owners = jnp.stack([(x + by) % nx for by in order]).astype(jnp.int32)
    piece_spec = spec((rows, band))
    bf_piece = jax.ShapeDtypeStruct((rows, band), bf16)
    own, *pieces = pl.pallas_call(
        add_kernel,
        grid_spec=pltpu.PrefetchScalarGridSpec(
            num_scalar_prefetch=1,
            grid=(nx,),
            in_specs=[
                pl.BlockSpec((rows, band), lambda i, s: (0, s[nx + i])),
                pl.BlockSpec((1, rows, band), lambda i, s: (s[i], 0, 0)),
            ],
            out_specs=[piece_spec] * nx,
        ),
        out_shape=[jax.ShapeDtypeStruct((rows, band), f32)] + [bf_piece] * (nx - 1),
        cost_estimate=pl.CostEstimate(
            flops=rows * cols // 2, bytes_accessed=4 * rows * cols, transcendentals=0
        ),
        compiler_params=params,
        name="add_cores",
    )(jnp.concatenate([owners, 2 * owners + core]).astype(jnp.int32), grad, got)
    pieces = [shift(value, "x", by) for by, value in zip(order, pieces)]
    return pl.pallas_call(
        total_kernel,
        grid_spec=pltpu.PrefetchScalarGridSpec(
            num_scalar_prefetch=1,
            grid=(1,),
            in_specs=[piece_spec] * nx,
            out_specs=spec((nblocks, piece, block)),
        ),
        out_shape=jax.ShapeDtypeStruct((nblocks, piece, block), bf16),
        cost_estimate=pl.CostEstimate(
            flops=3 * rows * band, bytes_accessed=6 * rows * band * 2, transcendentals=0
        ),
        compiler_params=params,
        name="total_in_slots",
    )(table, own, *pieces)


def settle_kernel(table, back, left, right, left_new, right_new, update):
    nz, _, per, piece, block = back.shape
    ncb = update.shape[1] // block
    for arr, stat, new in ((0, left, left_new), (1, right, right_new)):
        gram = back[:, arr].astype(f32).reshape(nz * per, piece, block)
        new[...] = (decay * stat[...].astype(f32) + gram).astype(bf16)
    for rb in range(0, update.shape[0] // piece, 2):
        for cb in range(ncb):
            pair = []
            for k in (rb * ncb + cb, (rb + 1) * ncb + cb):
                slot = table[k]
                pair.append(back[slot // per, 2, slot % per].astype(f32))
            update[rb * piece : (rb + 2) * piece, cb * block : (cb + 1) * block] = jnp.concatenate(
                pair, 0
            ).astype(bf16)


def settle(table, back, left, right, rows, cols):
    whole = lambda shape: pl.BlockSpec(shape, lambda i, t: (0,) * len(shape))
    return pl.pallas_call(
        settle_kernel,
        grid_spec=pltpu.PrefetchScalarGridSpec(
            num_scalar_prefetch=1,
            grid=(1,),
            in_specs=[whole(back.shape), whole(left.shape), whole(right.shape)],
            out_specs=[whole(left.shape), whole(right.shape), whole((rows, cols))],
        ),
        out_shape=[
            jax.ShapeDtypeStruct(left.shape, bf16),
            jax.ShapeDtypeStruct(right.shape, bf16),
            jax.ShapeDtypeStruct((rows, cols), bf16),
        ],
        cost_estimate=pl.CostEstimate(
            flops=4 * left.size, bytes_accessed=8 * left.size * 2, transcendentals=0
        ),
        compiler_params=params,
        name="settle",
    )(table, back, left, right)


def products_kernel(where, *refs):
    g_parts, (left_root, right_root, back, rows, gram) = refs[:4], refs[4:]
    nz, _, _, piece, block = back.shape
    ny = len(g_parts)
    y = where[0]
    scale = (1.0 - decay) / block

    def flat(value):
        return value.astype(f32).reshape(nz * piece, block).astype(bf16)

    def dot(a, b, over=((1,), (0,))):
        return lax.dot_general(a, b, (over, ((), ())), preferred_element_type=f32)

    for by, part in enumerate(g_parts):
        rows[:, lax.rem(y - by + ny, ny)] = part[:, 0].astype(f32)
    g = rows[...].reshape(block, block).astype(bf16)
    half = dot(flat(left_root[:, 0, 0]), g).astype(bf16)
    back[:, 2, 0] = dot(half, right_root[0]).reshape(nz, piece, block).astype(bf16)
    left = dot(flat(g_parts[0][:, 0]), g, ((1,), (1,)))
    back[:, 0, 0] = (scale * left).reshape(nz, piece, block).astype(bf16)
    gram[...] = dot(g, g, ((0,), (0,))).reshape(gram.shape)
    back[:, 1, 0] = (scale * gram[:, y]).astype(bf16)


def products(g_parts, roots, right_root, y):
    ny = len(g_parts)
    nz, per, piece, block = g_parts[0].shape
    part = pl.BlockSpec((nz, 1, piece, block), lambda s, _: (0, s, 0, 0))
    several = lambda n: pl.BlockSpec((nz, n, 1, piece, block), lambda s, _: (0, 0, s, 0, 0))
    return pl.pallas_call(
        products_kernel,
        grid_spec=pltpu.PrefetchScalarGridSpec(
            num_scalar_prefetch=1,
            grid=(per,),
            in_specs=[part] * ny + [several(1), pl.BlockSpec((1, block, block), lambda s, _: (s, 0, 0))],
            out_specs=several(3),
            scratch_shapes=[pltpu.VMEM((nz, ny, piece, block), f32)] * 2,
        ),
        out_shape=jax.ShapeDtypeStruct((nz, 3, per, piece, block), bf16),
        cost_estimate=pl.CostEstimate(
            flops=4 * per * block**3, bytes_accessed=24 * per * block * block, transcendentals=0
        ),
        compiler_params=wide,
        name="products",
    )(y.astype(jnp.int32).reshape(1), *g_parts, roots, right_root)


def local(grad_parts, slot_table, left_stat, right_stat, left_root, right_root):
    nz, ny = lax.axis_size("z"), lax.axis_size("y")
    y = lax.axis_index("y")
    nblocks, piece, block = left_stat.shape[1:]
    rows_dev = grad_parts.shape[1]
    ncb = nblocks // (rows_dev // piece)
    per = nblocks // nz
    table = slot_table[0]
    by_owner = (nz, per, piece, block)

    def to_owner(value):
        return lax.all_to_all(value, "z", 0, 0, tiled=True)

    def from_y(value):
        far = [shift(value, "y", by) for by in (2, 1, 3)]
        return [value, far[1], far[0], far[2]]

    roots = to_owner(stack_roots(left_root[0].reshape(by_owner), right_root[0].reshape(by_owner)))
    placed = sum_dp(grad_parts[0], table, nblocks, piece, block)
    grads = to_owner(placed.reshape(by_owner))
    right = from_y(roots[:, 1])
    right = jnp.stack([lax.select_n((y - owner) % ny, *right) for owner in range(ny)])
    right = right.transpose(2, 1, 0, 3, 4).reshape(per, block, block)
    back = products(from_y(grads), roots, right, y)
    back = lax.all_to_all(back, "z", 0, 0, tiled=True)
    left_new, right_new, update = settle(
        table, back, left_stat[0], right_stat[0], rows_dev, ncb * block
    )
    return left_new[None], right_new[None], update


def solution(mesh):
    ny = 4
    devices = mesh.devices
    split = Mesh(
        devices.reshape(devices.shape[0] // 2, 2, devices.shape[1] // ny, ny), ("x", "core", "z", "y")
    )
    dp, fsdp = ("x", "core"), ("z", "y")
    factor = P(dp, None, fsdp, None)
    return jax.shard_map(
        local,
        mesh=split,
        in_specs=(P(dp, fsdp, None), P(dp, None), factor, factor, factor, factor),
        out_specs=(factor, factor, P(fsdp, dp)),
        check_vma=False,
    )
```

```python
import jax
import jax.numpy as jnp
from jax import lax
from jax.experimental import pallas as pl
from jax.experimental.pallas import tpu as pltpu
from jax.sharding import Mesh, PartitionSpec as P

decay = 0.9
bf16 = jnp.bfloat16
f32 = jnp.float32
params = pltpu.CompilerParams(vmem_limit_bytes=12 * 1024 * 1024)


def shift(value, axis, by):
    n = lax.axis_size(axis)
    return lax.ppermute(value, axis, [(i, (i + by) % n) for i in range(n)])


def add_kernel(where, grad, got, own, *outs):
    step = pl.program_id(0)
    total = grad[...].astype(f32) + got[...].astype(f32)
    for i, out in enumerate(outs):

        @pl.when(step == i)
        def _():
            out[...] = total.astype(bf16)

    @pl.when(step == len(outs))
    def _():
        own[...] = total


def total_kernel(table, own, first, second, third, out):
    nblocks, piece, block = out.shape
    ncb = own.shape[1] // block
    total = own[...] + first[...].astype(f32) + second[...].astype(f32) + third[...].astype(f32)
    for k in range(nblocks):
        row, col = k // ncb * piece, k % ncb * block
        out[table[k]] = total[row : row + piece, col : col + block].astype(bf16)


def spec(shape):
    return pl.BlockSpec(shape, lambda *_: (0,) * len(shape))


def sum_dp(grad, table, nblocks, piece, block):
    nx = lax.axis_size("x")
    core = lax.axis_index("core")
    x = lax.axis_index("x")
    rows, cols = grad.shape
    band = cols // (2 * nx)
    got = lax.ppermute(grad, "core", [(0, 1), (1, 0)])

    order = (2, 1, 3, 0)
    owners = jnp.stack([(x + by) % nx for by in order]).astype(jnp.int32)
    piece_spec = spec((rows, band))
    bf_piece = jax.ShapeDtypeStruct((rows, band), bf16)
    own, *pieces = pl.pallas_call(
        add_kernel,
        grid_spec=pltpu.PrefetchScalarGridSpec(
            num_scalar_prefetch=1,
            grid=(nx,),
            in_specs=[
                pl.BlockSpec((rows, band), lambda i, s: (0, s[nx + i])),
                pl.BlockSpec((rows, band), lambda i, s: (0, s[nx + i])),
            ],
            out_specs=[piece_spec] * nx,
        ),
        out_shape=[jax.ShapeDtypeStruct((rows, band), f32)] + [bf_piece] * (nx - 1),
        cost_estimate=pl.CostEstimate(
            flops=rows * cols // 2, bytes_accessed=4 * rows * cols, transcendentals=0
        ),
        compiler_params=params,
        name="add_cores",
    )(jnp.concatenate([owners, 2 * owners + core]).astype(jnp.int32), grad, got)
    pieces = [shift(value, "x", by) for by, value in zip(order, pieces)]
    return pl.pallas_call(
        total_kernel,
        grid_spec=pltpu.PrefetchScalarGridSpec(
            num_scalar_prefetch=1,
            grid=(1,),
            in_specs=[piece_spec] * nx,
            out_specs=spec((nblocks, piece, block)),
        ),
        out_shape=jax.ShapeDtypeStruct((nblocks, piece, block), bf16),
        cost_estimate=pl.CostEstimate(
            flops=3 * rows * band, bytes_accessed=6 * rows * band * 2, transcendentals=0
        ),
        compiler_params=params,
        name="total_in_slots",
    )(table, own, *pieces)


def settle_kernel(table, back, left, right, left_new, right_new, update):
    nz, _, per, piece, block = back.shape
    ncb = update.shape[1] // block
    for arr, stat, new in ((0, left, left_new), (1, right, right_new)):
        gram = back[:, arr].astype(f32).reshape(nz * per, piece, block)
        new[...] = (decay * stat[...].astype(f32) + gram).astype(bf16)
    for rb in range(0, update.shape[0] // piece, 2):
        for cb in range(ncb):
            pair = []
            for k in (rb * ncb + cb, (rb + 1) * ncb + cb):
                slot = table[k]
                pair.append(back[slot // per, 2, slot % per].astype(f32))
            update[rb * piece : (rb + 2) * piece, cb * block : (cb + 1) * block] = jnp.concatenate(
                pair, 0
            ).astype(bf16)


def settle(table, back, left, right, rows, cols):
    whole = lambda shape: pl.BlockSpec(shape, lambda i, t: (0,) * len(shape))
    return pl.pallas_call(
        settle_kernel,
        grid_spec=pltpu.PrefetchScalarGridSpec(
            num_scalar_prefetch=1,
            grid=(1,),
            in_specs=[whole(back.shape), whole(left.shape), whole(right.shape)],
            out_specs=[whole(left.shape), whole(right.shape), whole((rows, cols))],
        ),
        out_shape=[
            jax.ShapeDtypeStruct(left.shape, bf16),
            jax.ShapeDtypeStruct(right.shape, bf16),
            jax.ShapeDtypeStruct((rows, cols), bf16),
        ],
        cost_estimate=pl.CostEstimate(
            flops=4 * left.size, bytes_accessed=8 * left.size * 2, transcendentals=0
        ),
        compiler_params=params,
        name="settle",
    )(table, back, left, right)


def products_kernel(where, *refs):
    g_parts, (left_root, right_root, back, rows, gram) = refs[:4], refs[4:]
    nz, _, _, piece, block = back.shape
    ny = len(g_parts)
    y = where[0]
    scale = (1.0 - decay) / block

    def flat(value):
        return value.astype(f32).reshape(nz * piece, block).astype(bf16)

    def dot(a, b, over=((1,), (0,))):
        return lax.dot_general(a, b, (over, ((), ())), preferred_element_type=f32)

    for by, part in enumerate(g_parts):
        rows[:, lax.rem(y - by + ny, ny)] = part[:, 0].astype(f32)
    g = rows[...].reshape(block, block).astype(bf16)
    half = dot(flat(left_root[:, 0, 0]), g).astype(bf16)
    back[:, 2, 0] = dot(half, right_root[0]).reshape(nz, piece, block).astype(bf16)
    left = dot(flat(g_parts[0][:, 0]), g, ((1,), (1,)))
    back[:, 0, 0] = (scale * left).reshape(nz, piece, block).astype(bf16)
    gram[...] = dot(g, g, ((0,), (0,))).reshape(gram.shape)
    back[:, 1, 0] = (scale * gram[:, y]).astype(bf16)


def products(g_parts, roots, right_root, y):
    ny = len(g_parts)
    nz, per, piece, block = g_parts[0].shape
    part = pl.BlockSpec((nz, 1, piece, block), lambda s, _: (0, s, 0, 0))
    several = lambda n: pl.BlockSpec((nz, n, 1, piece, block), lambda s, _: (0, 0, s, 0, 0))
    return pl.pallas_call(
        products_kernel,
        grid_spec=pltpu.PrefetchScalarGridSpec(
            num_scalar_prefetch=1,
            grid=(per,),
            in_specs=[part] * ny + [several(1), pl.BlockSpec((1, block, block), lambda s, _: (s, 0, 0))],
            out_specs=several(3),
            scratch_shapes=[pltpu.VMEM((nz, ny, piece, block), f32)] * 2,
        ),
        out_shape=jax.ShapeDtypeStruct((nz, 3, per, piece, block), bf16),
        cost_estimate=pl.CostEstimate(
            flops=4 * per * block**3, bytes_accessed=24 * per * block * block, transcendentals=0
        ),
        compiler_params=params,
        name="products",
    )(y.astype(jnp.int32).reshape(1), *g_parts, roots, right_root)


def local(grad_parts, slot_table, left_stat, right_stat, left_root, right_root):
    nz, ny = lax.axis_size("z"), lax.axis_size("y")
    y = lax.axis_index("y")
    nblocks, piece, block = left_stat.shape[1:]
    rows_dev = grad_parts.shape[1]
    ncb = nblocks // (rows_dev // piece)
    per = nblocks // nz
    table = slot_table[0]
    by_owner = (nz, per, piece, block)

    def to_owner(value):
        return lax.all_to_all(value, "z", 0, 0, tiled=True)

    def from_y(value):
        far = [shift(value, "y", by) for by in (2, 1, 3)]
        return [value, far[1], far[0], far[2]]

    roots = to_owner(jnp.stack([left_root[0].reshape(by_owner), right_root[0].reshape(by_owner)], 1))
    placed = sum_dp(grad_parts[0], table, nblocks, piece, block)
    grads = to_owner(placed.reshape(by_owner))
    right = from_y(roots[:, 1])
    right = jnp.stack([lax.select_n((y - owner) % ny, *right) for owner in range(ny)])
    right = right.transpose(2, 1, 0, 3, 4).reshape(per, block, block)
    back = products(from_y(grads), roots, right, y)
    back = lax.all_to_all(back, "z", 0, 0, tiled=True)
    left_new, right_new, update = settle(
        table, back, left_stat[0], right_stat[0], rows_dev, ncb * block
    )
    return left_new[None], right_new[None], update


def solution(mesh):
    ny = 4
    devices = mesh.devices
    split = Mesh(
        devices.reshape(devices.shape[0] // 2, 2, devices.shape[1] // ny, ny), ("x", "core", "z", "y")
    )
    dp, fsdp = ("x", "core"), ("z", "y")
    factor = P(dp, None, fsdp, None)
    return jax.shard_map(
        local,
        mesh=split,
        in_specs=(P(dp, fsdp, None), P(dp, None), factor, factor, factor, factor),
        out_specs=(factor, factor, P(fsdp, dp)),
        check_vma=False,
    )
```

```python
import jax
import jax.numpy as jnp
from jax import lax
from jax.experimental import pallas as pl
from jax.experimental.pallas import tpu as pltpu
from jax.sharding import Mesh, PartitionSpec as P

decay = 0.9
bf16 = jnp.bfloat16
f32 = jnp.float32
params = pltpu.CompilerParams(vmem_limit_bytes=12 * 1024 * 1024)


def shift(value, axis, by):
    n = lax.axis_size(axis)
    return lax.ppermute(value, axis, [(i, (i + by) % n) for i in range(n)])


def add_kernel(where, grad, got, own, *outs):
    step = pl.program_id(0)
    total = grad[...].astype(f32) + got[...].astype(f32)
    for i, out in enumerate(outs):

        @pl.when(step == i)
        def _():
            out[...] = total.astype(bf16)

    @pl.when(step == len(outs))
    def _():
        own[...] = total


def total_kernel(table, own, first, second, third, out):
    nblocks, piece, block = out.shape
    ncb = own.shape[1] // block
    total = own[...] + first[...].astype(f32) + second[...].astype(f32) + third[...].astype(f32)
    for k in range(nblocks):
        row, col = k // ncb * piece, k % ncb * block
        out[table[k]] = total[row : row + piece, col : col + block].astype(bf16)


def spec(shape):
    return pl.BlockSpec(shape, lambda *_: (0,) * len(shape))


def sum_dp(grad, table, nblocks, piece, block):
    nx = lax.axis_size("x")
    core = lax.axis_index("core")
    x = lax.axis_index("x")
    rows, cols = grad.shape
    band = cols // (2 * nx)
    got = lax.ppermute(grad, "core", [(0, 1), (1, 0)])

    order = (2, 1, 3, 0)
    owners = jnp.stack([(x + by) % nx for by in order]).astype(jnp.int32)
    piece_spec = spec((rows, band))
    bf_piece = jax.ShapeDtypeStruct((rows, band), bf16)
    own, *pieces = pl.pallas_call(
        add_kernel,
        grid_spec=pltpu.PrefetchScalarGridSpec(
            num_scalar_prefetch=1,
            grid=(nx,),
            in_specs=[
                pl.BlockSpec((rows, band), lambda i, s: (0, s[nx + i])),
                pl.BlockSpec((rows, band), lambda i, s: (0, s[nx + i])),
            ],
            out_specs=[piece_spec] * nx,
        ),
        out_shape=[jax.ShapeDtypeStruct((rows, band), f32)] + [bf_piece] * (nx - 1),
        cost_estimate=pl.CostEstimate(
            flops=rows * cols // 2, bytes_accessed=4 * rows * cols, transcendentals=0
        ),
        compiler_params=params,
        name="add_cores",
    )(jnp.concatenate([owners, 2 * owners + core]).astype(jnp.int32), grad, got)
    pieces = [shift(value, "x", by) for by, value in zip(order, pieces)]
    return pl.pallas_call(
        total_kernel,
        grid_spec=pltpu.PrefetchScalarGridSpec(
            num_scalar_prefetch=1,
            grid=(1,),
            in_specs=[piece_spec] * nx,
            out_specs=spec((nblocks, piece, block)),
        ),
        out_shape=jax.ShapeDtypeStruct((nblocks, piece, block), bf16),
        cost_estimate=pl.CostEstimate(
            flops=3 * rows * band, bytes_accessed=6 * rows * band * 2, transcendentals=0
        ),
        compiler_params=params,
        name="total_in_slots",
    )(table, own, *pieces)


def settle_kernel(table, back, left, right, left_new, right_new, update):
    nz, _, per, piece, block = back.shape
    ncb = update.shape[1] // block
    for arr, stat, new in ((0, left, left_new), (1, right, right_new)):
        gram = back[:, arr].astype(f32).reshape(nz * per, piece, block)
        new[...] = (stat[...] + gram).astype(bf16)
    for rb in range(0, update.shape[0] // piece, 2):
        for cb in range(ncb):
            pair = []
            for k in (rb * ncb + cb, (rb + 1) * ncb + cb):
                slot = table[k]
                pair.append(back[slot // per, 2, slot % per].astype(f32))
            update[rb * piece : (rb + 2) * piece, cb * block : (cb + 1) * block] = jnp.concatenate(
                pair, 0
            ).astype(bf16)


def settle(table, back, left, right, rows, cols):
    whole = lambda shape: pl.BlockSpec(shape, lambda i, t: (0,) * len(shape))
    return pl.pallas_call(
        settle_kernel,
        grid_spec=pltpu.PrefetchScalarGridSpec(
            num_scalar_prefetch=1,
            grid=(1,),
            in_specs=[whole(back.shape), whole(left.shape), whole(right.shape)],
            out_specs=[whole(left.shape), whole(right.shape), whole((rows, cols))],
        ),
        out_shape=[
            jax.ShapeDtypeStruct(left.shape, bf16),
            jax.ShapeDtypeStruct(right.shape, bf16),
            jax.ShapeDtypeStruct((rows, cols), bf16),
        ],
        cost_estimate=pl.CostEstimate(
            flops=4 * left.size, bytes_accessed=8 * left.size * 2, transcendentals=0
        ),
        compiler_params=params,
        name="settle",
    )(table, back, left, right)


def products_kernel(where, *refs):
    g_parts, (left_root, right_root, back, rows, gram) = refs[:4], refs[4:]
    nz, _, _, piece, block = back.shape
    ny = len(g_parts)
    y = where[0]
    scale = (1.0 - decay) / block

    def flat(value):
        return value.astype(f32).reshape(nz * piece, block).astype(bf16)

    def dot(a, b, over=((1,), (0,))):
        return lax.dot_general(a, b, (over, ((), ())), preferred_element_type=f32)

    for by, part in enumerate(g_parts):
        rows[:, lax.rem(y - by + ny, ny)] = part[:, 0].astype(f32)
    g = rows[...].reshape(block, block).astype(bf16)
    half = dot(flat(left_root[:, 0, 0]), g).astype(bf16)
    back[:, 2, 0] = dot(half, right_root[0]).reshape(nz, piece, block).astype(bf16)
    left = dot(flat(g_parts[0][:, 0]), g, ((1,), (1,)))
    back[:, 0, 0] = (scale * left).reshape(nz, piece, block).astype(bf16)
    gram[...] = dot(g, g, ((0,), (0,))).reshape(gram.shape)
    back[:, 1, 0] = (scale * gram[:, y]).astype(bf16)


def products(g_parts, roots, right_root, y):
    ny = len(g_parts)
    nz, per, piece, block = g_parts[0].shape
    part = pl.BlockSpec((nz, 1, piece, block), lambda s, _: (0, s, 0, 0))
    several = lambda n: pl.BlockSpec((nz, n, 1, piece, block), lambda s, _: (0, 0, s, 0, 0))
    return pl.pallas_call(
        products_kernel,
        grid_spec=pltpu.PrefetchScalarGridSpec(
            num_scalar_prefetch=1,
            grid=(per,),
            in_specs=[part] * ny + [several(1), pl.BlockSpec((1, block, block), lambda s, _: (s, 0, 0))],
            out_specs=several(3),
            scratch_shapes=[pltpu.VMEM((nz, ny, piece, block), f32)] * 2,
        ),
        out_shape=jax.ShapeDtypeStruct((nz, 3, per, piece, block), bf16),
        cost_estimate=pl.CostEstimate(
            flops=4 * per * block**3, bytes_accessed=24 * per * block * block, transcendentals=0
        ),
        compiler_params=params,
        name="products",
    )(y.astype(jnp.int32).reshape(1), *g_parts, roots, right_root)


def local(grad_parts, slot_table, left_stat, right_stat, left_root, right_root):
    nz, ny = lax.axis_size("z"), lax.axis_size("y")
    y = lax.axis_index("y")
    nblocks, piece, block = left_stat.shape[1:]
    rows_dev = grad_parts.shape[1]
    ncb = nblocks // (rows_dev // piece)
    per = nblocks // nz
    table = slot_table[0]
    by_owner = (nz, per, piece, block)

    def to_owner(value):
        return lax.all_to_all(value, "z", 0, 0, tiled=True)

    def from_y(value):
        far = [shift(value, "y", by) for by in (2, 1, 3)]
        return [value, far[1], far[0], far[2]]

    roots = to_owner(jnp.stack([left_root[0].reshape(by_owner), right_root[0].reshape(by_owner)], 1))
    placed = sum_dp(grad_parts[0], table, nblocks, piece, block)
    grads = to_owner(placed.reshape(by_owner))
    right = from_y(roots[:, 1])
    right = jnp.stack([lax.select_n((y - owner) % ny, *right) for owner in range(ny)])
    right = right.transpose(2, 1, 0, 3, 4).reshape(per, block, block)
    back = products(from_y(grads), roots, right, y)
    back, left_stat, right_stat = lax.optimization_barrier((back, left_stat, right_stat))
    back = lax.all_to_all(back, "z", 0, 0, tiled=True)
    left_stat, right_stat = (decay * left_stat.astype(f32), decay * right_stat.astype(f32))
    left_new, right_new, update = settle(
        table, back, left_stat[0], right_stat[0], rows_dev, ncb * block
    )
    return left_new[None], right_new[None], update


def solution(mesh):
    ny = 4
    devices = mesh.devices
    split = Mesh(
        devices.reshape(devices.shape[0] // 2, 2, devices.shape[1] // ny, ny), ("x", "core", "z", "y")
    )
    dp, fsdp = ("x", "core"), ("z", "y")
    factor = P(dp, None, fsdp, None)
    return jax.shard_map(
        local,
        mesh=split,
        in_specs=(P(dp, fsdp, None), P(dp, None), factor, factor, factor, factor),
        out_specs=(factor, factor, P(fsdp, dp)),
        check_vma=False,
    )
```

```python
import jax
import jax.numpy as jnp
from jax import lax
from jax.experimental import pallas as pl
from jax.experimental.pallas import tpu as pltpu
from jax.sharding import Mesh, PartitionSpec as P

decay = 0.9
bf16 = jnp.bfloat16
f32 = jnp.float32
params = pltpu.CompilerParams(vmem_limit_bytes=12 * 1024 * 1024)


def shift(value, axis, by):
    n = lax.axis_size(axis)
    return lax.ppermute(value, axis, [(i, (i + by) % n) for i in range(n)])


def stack_kernel(left, right, out):
    out[:, 0] = left[...]
    out[:, 1] = right[...]


def add_kernel(where, grad, got, own, *refs):
    outs, (mine, theirs, sems) = refs[:-3], refs[-3:]
    count, _, band = mine.shape
    copies = []
    for i in range(count):
        columns = pl.ds(pl.multiple_of(where[i] * band, band), band)
        copies.append(
            (
                pltpu.make_async_copy(grad.at[:, columns], mine.at[i], sems.at[0, i]),
                pltpu.make_async_copy(got.at[:, columns], theirs.at[i], sems.at[1, i]),
            )
        )
        for copy in copies[i]:
            copy.start()
    for i in range(count):
        for copy in copies[i]:
            copy.wait()
        total = mine[i].astype(f32) + theirs[i].astype(f32)
        if i < len(outs):
            outs[i][...] = total.astype(bf16)
        else:
            own[...] = total


def total_kernel(table, own, first, second, third, out):
    nblocks, piece, block = out.shape
    ncb = own.shape[1] // block
    total = own[...] + first[...].astype(f32) + second[...].astype(f32) + third[...].astype(f32)
    for k in range(nblocks):
        row, col = k // ncb * piece, k % ncb * block
        out[table[k]] = total[row : row + piece, col : col + block].astype(bf16)


def spec(shape):
    return pl.BlockSpec(shape, lambda *_: (0,) * len(shape))


def stack_roots(left, right):
    nz, per, piece, block = left.shape
    return pl.pallas_call(
        stack_kernel,
        grid=(2,),
        in_specs=[pl.BlockSpec((nz // 2, per, piece, block), lambda i: (i, 0, 0, 0))] * 2,
        out_specs=pl.BlockSpec((nz // 2, 2, per, piece, block), lambda i: (i, 0, 0, 0, 0)),
        out_shape=jax.ShapeDtypeStruct((nz, 2, per, piece, block), bf16),
        cost_estimate=pl.CostEstimate(flops=0, bytes_accessed=8 * left.size, transcendentals=0),
        compiler_params=params,
        name="stack_roots",
    )(left, right)


def sum_dp(grad, table, nblocks, piece, block):
    nx = lax.axis_size("x")
    core = lax.axis_index("core")
    x = lax.axis_index("x")
    rows, cols = grad.shape
    band = cols // (2 * nx)
    got = lax.ppermute(grad, "core", [(0, 1), (1, 0)])

    order = (2, 1, 3, 0)
    owners = jnp.stack([(x + by) % nx for by in order]).astype(jnp.int32)
    piece_spec = spec((rows, band))
    bf_piece = jax.ShapeDtypeStruct((rows, band), bf16)
    own, *pieces = pl.pallas_call(
        add_kernel,
        grid_spec=pltpu.PrefetchScalarGridSpec(
            num_scalar_prefetch=1,
            grid=(1,),
            in_specs=[pl.BlockSpec(memory_space=pltpu.HBM)] * 2,
            out_specs=[piece_spec] * nx,
            scratch_shapes=[pltpu.VMEM((nx, rows, band), bf16)] * 2 + [pltpu.SemaphoreType.DMA((2, nx))],
        ),
        out_shape=[jax.ShapeDtypeStruct((rows, band), f32)] + [bf_piece] * (nx - 1),
        cost_estimate=pl.CostEstimate(
            flops=rows * cols // 2, bytes_accessed=4 * rows * cols, transcendentals=0
        ),
        compiler_params=params,
        name="add_cores",
    )(2 * owners + core, grad, got)
    pieces = [shift(value, "x", by) for by, value in zip(order, pieces)]
    return pl.pallas_call(
        total_kernel,
        grid_spec=pltpu.PrefetchScalarGridSpec(
            num_scalar_prefetch=1,
            grid=(1,),
            in_specs=[piece_spec] * nx,
            out_specs=spec((nblocks, piece, block)),
        ),
        out_shape=jax.ShapeDtypeStruct((nblocks, piece, block), bf16),
        cost_estimate=pl.CostEstimate(
            flops=3 * rows * band, bytes_accessed=6 * rows * band * 2, transcendentals=0
        ),
        compiler_params=params,
        name="total_in_slots",
    )(table, own, *pieces)


def settle_kernel(table, back, left, right, left_new, right_new, update):
    nz, _, per, piece, block = back.shape
    ncb = update.shape[1] // block
    for arr, stat, new in ((0, left, left_new), (1, right, right_new)):
        gram = back[:, arr].astype(f32).reshape(nz * per, piece, block)
        new[...] = (stat[...] + gram).astype(bf16)
    for rb in range(0, update.shape[0] // piece, 2):
        for cb in range(ncb):
            pair = []
            for k in (rb * ncb + cb, (rb + 1) * ncb + cb):
                slot = table[k]
                pair.append(back[slot // per, 2, slot % per].astype(f32))
            update[rb * piece : (rb + 2) * piece, cb * block : (cb + 1) * block] = jnp.concatenate(
                pair, 0
            ).astype(bf16)


def settle(table, back, left, right, rows, cols):
    whole = lambda shape: pl.BlockSpec(shape, lambda i, t: (0,) * len(shape))
    return pl.pallas_call(
        settle_kernel,
        grid_spec=pltpu.PrefetchScalarGridSpec(
            num_scalar_prefetch=1,
            grid=(1,),
            in_specs=[whole(back.shape), whole(left.shape), whole(right.shape)],
            out_specs=[whole(left.shape), whole(right.shape), whole((rows, cols))],
        ),
        out_shape=[
            jax.ShapeDtypeStruct(left.shape, bf16),
            jax.ShapeDtypeStruct(right.shape, bf16),
            jax.ShapeDtypeStruct((rows, cols), bf16),
        ],
        cost_estimate=pl.CostEstimate(
            flops=4 * left.size, bytes_accessed=8 * left.size * 2, transcendentals=0
        ),
        compiler_params=params,
        name="settle",
    )(table, back, left, right)


def products_kernel(where, *refs):
    g_parts, (left_root, right_root, back, rows, gram) = refs[:4], refs[4:]
    nz, _, _, piece, block = back.shape
    ny = len(g_parts)
    y = where[0]
    scale = (1.0 - decay) / block

    def flat(value):
        return value.astype(f32).reshape(nz * piece, block).astype(bf16)

    def dot(a, b, over=((1,), (0,))):
        return lax.dot_general(a, b, (over, ((), ())), preferred_element_type=f32)

    for by, part in enumerate(g_parts):
        rows[:, lax.rem(y - by + ny, ny)] = part[:, 0].astype(f32)
    g = rows[...].reshape(block, block).astype(bf16)
    half = dot(flat(left_root[:, 0, 0]), g).astype(bf16)
    back[:, 2, 0] = dot(half, right_root[0]).reshape(nz, piece, block).astype(bf16)
    left = dot(flat(g_parts[0][:, 0]), g, ((1,), (1,)))
    back[:, 0, 0] = (scale * left).reshape(nz, piece, block).astype(bf16)
    gram[...] = dot(g, g, ((0,), (0,))).reshape(gram.shape)
    back[:, 1, 0] = (scale * gram[:, y]).astype(bf16)


def products(g_parts, roots, right_root, y):
    ny = len(g_parts)
    nz, per, piece, block = g_parts[0].shape
    part = pl.BlockSpec((nz, 1, piece, block), lambda s, _: (0, s, 0, 0))
    several = lambda n: pl.BlockSpec((nz, n, 1, piece, block), lambda s, _: (0, 0, s, 0, 0))
    return pl.pallas_call(
        products_kernel,
        grid_spec=pltpu.PrefetchScalarGridSpec(
            num_scalar_prefetch=1,
            grid=(per,),
            in_specs=[part] * ny + [several(1), pl.BlockSpec((1, block, block), lambda s, _: (s, 0, 0))],
            out_specs=several(3),
            scratch_shapes=[pltpu.VMEM((nz, ny, piece, block), f32)] * 2,
        ),
        out_shape=jax.ShapeDtypeStruct((nz, 3, per, piece, block), bf16),
        cost_estimate=pl.CostEstimate(
            flops=4 * per * block**3, bytes_accessed=24 * per * block * block, transcendentals=0
        ),
        compiler_params=params,
        name="products",
    )(y.astype(jnp.int32).reshape(1), *g_parts, roots, right_root)


def local(grad_parts, slot_table, left_stat, right_stat, left_root, right_root):
    nz, ny = lax.axis_size("z"), lax.axis_size("y")
    y = lax.axis_index("y")
    nblocks, piece, block = left_stat.shape[1:]
    rows_dev = grad_parts.shape[1]
    ncb = nblocks // (rows_dev // piece)
    per = nblocks // nz
    table = slot_table[0]
    by_owner = (nz, per, piece, block)

    def to_owner(value):
        return lax.all_to_all(value, "z", 0, 0, tiled=True)

    def from_y(value):
        far = [shift(value, "y", by) for by in (2, 1, 3)]
        return [value, far[1], far[0], far[2]]

    roots = to_owner(jnp.stack([left_root[0].reshape(by_owner), right_root[0].reshape(by_owner)], 1))
    placed = sum_dp(grad_parts[0], table, nblocks, piece, block)
    grads = to_owner(placed.reshape(by_owner))
    right = from_y(roots[:, 1])
    right = jnp.stack([lax.select_n((y - owner) % ny, *right) for owner in range(ny)])
    right = right.transpose(2, 1, 0, 3, 4).reshape(per, block, block)
    back = products(from_y(grads), roots, right, y)
    back, left_stat, right_stat = lax.optimization_barrier((back, left_stat, right_stat))
    back = lax.all_to_all(back, "z", 0, 0, tiled=True)
    left_stat, right_stat = (decay * left_stat.astype(f32), decay * right_stat.astype(f32))
    left_new, right_new, update = settle(
        table, back, left_stat[0], right_stat[0], rows_dev, ncb * block
    )
    return left_new[None], right_new[None], update


def solution(mesh):
    ny = 4
    devices = mesh.devices
    split = Mesh(
        devices.reshape(devices.shape[0] // 2, 2, devices.shape[1] // ny, ny), ("x", "core", "z", "y")
    )
    dp, fsdp = ("x", "core"), ("z", "y")
    factor = P(dp, None, fsdp, None)
    return jax.shard_map(
        local,
        mesh=split,
        in_specs=(P(dp, fsdp, None), P(dp, None), factor, factor, factor, factor),
        out_specs=(factor, factor, P(fsdp, dp)),
        check_vma=False,
    )
```

```python
import jax
import jax.numpy as jnp
from jax import lax
from jax.experimental import pallas as pl
from jax.experimental.pallas import tpu as pltpu
from jax.sharding import Mesh, PartitionSpec as P

decay = 0.9
bf16 = jnp.bfloat16
f32 = jnp.float32
params = pltpu.CompilerParams(vmem_limit_bytes=12 * 1024 * 1024)


def shift(value, axis, by):
    n = lax.axis_size(axis)
    return lax.ppermute(value, axis, [(i, (i + by) % n) for i in range(n)])


def add_kernel(where, grad, got, own, *outs):
    step = pl.program_id(0)
    total = grad[...].astype(f32) + got[...].astype(f32)
    for i, out in enumerate(outs):

        @pl.when(step == i)
        def _():
            out[...] = total.astype(bf16)

    @pl.when(step == len(outs))
    def _():
        own[...] = total


def total_kernel(table, own, first, second, third, out):
    nblocks, piece, block = out.shape
    ncb = own.shape[1] // block
    total = own[...] + first[...].astype(f32) + second[...].astype(f32) + third[...].astype(f32)
    for k in range(nblocks):
        row, col = k // ncb * piece, k % ncb * block
        out[table[k]] = total[row : row + piece, col : col + block].astype(bf16)


def spec(shape):
    return pl.BlockSpec(shape, lambda *_: (0,) * len(shape))


def sum_dp(grad, table, nblocks, piece, block):
    nx = lax.axis_size("x")
    core = lax.axis_index("core")
    x = lax.axis_index("x")
    rows, cols = grad.shape
    band = cols // (2 * nx)
    got = lax.ppermute(grad, "core", [(0, 1), (1, 0)])

    order = (2, 1, 3, 0)
    owners = jnp.stack([(x + by) % nx for by in order]).astype(jnp.int32)
    piece_spec = spec((rows, band))
    bf_piece = jax.ShapeDtypeStruct((rows, band), bf16)
    own, *pieces = pl.pallas_call(
        add_kernel,
        grid_spec=pltpu.PrefetchScalarGridSpec(
            num_scalar_prefetch=1,
            grid=(nx,),
            in_specs=[
                pl.BlockSpec((rows, band), lambda i, s: (0, s[nx + i])),
                pl.BlockSpec((rows, band), lambda i, s: (0, s[nx + i])),
            ],
            out_specs=[piece_spec] * nx,
        ),
        out_shape=[jax.ShapeDtypeStruct((rows, band), f32)] + [bf_piece] * (nx - 1),
        cost_estimate=pl.CostEstimate(
            flops=rows * cols // 2, bytes_accessed=4 * rows * cols, transcendentals=0
        ),
        compiler_params=params,
        name="add_cores",
    )(jnp.concatenate([owners, 2 * owners + core]).astype(jnp.int32), grad, got)
    pieces = [shift(value, "x", by) for by, value in zip(order, pieces)]
    return pl.pallas_call(
        total_kernel,
        grid_spec=pltpu.PrefetchScalarGridSpec(
            num_scalar_prefetch=1,
            grid=(1,),
            in_specs=[piece_spec] * nx,
            out_specs=spec((nblocks, piece, block)),
        ),
        out_shape=jax.ShapeDtypeStruct((nblocks, piece, block), bf16),
        cost_estimate=pl.CostEstimate(
            flops=3 * rows * band, bytes_accessed=6 * rows * band * 2, transcendentals=0
        ),
        compiler_params=params,
        name="total_in_slots",
    )(table, own, *pieces)


def settle_kernel(table, back, left, right, left_new, right_new, update):
    nz, _, per, piece, block = back.shape
    ncb = update.shape[1] // block
    for arr, stat, new in ((0, left, left_new), (1, right, right_new)):
        gram = back[:, arr].astype(f32).reshape(nz * per, piece, block)
        new[...] = (stat[...] + gram).astype(bf16)
    for rb in range(0, update.shape[0] // piece, 2):
        for cb in range(ncb):
            pair = []
            for k in (rb * ncb + cb, (rb + 1) * ncb + cb):
                slot = table[k]
                pair.append(back[slot // per, 2, slot % per].astype(f32))
            update[rb * piece : (rb + 2) * piece, cb * block : (cb + 1) * block] = jnp.concatenate(
                pair, 0
            ).astype(bf16)


def settle(table, back, left, right, rows, cols):
    whole = lambda shape: pl.BlockSpec(shape, lambda i, t: (0,) * len(shape))
    return pl.pallas_call(
        settle_kernel,
        grid_spec=pltpu.PrefetchScalarGridSpec(
            num_scalar_prefetch=1,
            grid=(1,),
            in_specs=[pl.BlockSpec(memory_space=pltpu.VMEM)] * 3,
            out_specs=[whole(left.shape), whole(right.shape), whole((rows, cols))],
        ),
        out_shape=[
            jax.ShapeDtypeStruct(left.shape, bf16),
            jax.ShapeDtypeStruct(right.shape, bf16),
            jax.ShapeDtypeStruct((rows, cols), bf16),
        ],
        cost_estimate=pl.CostEstimate(
            flops=4 * left.size, bytes_accessed=8 * left.size * 2, transcendentals=0
        ),
        compiler_params=params,
        name="settle",
    )(table, back, left, right)


def products_kernel(where, *refs):
    g_parts, (left_root, right_root, back, rows, gram) = refs[:4], refs[4:]
    nz, _, _, piece, block = back.shape
    ny = len(g_parts)
    y = where[0]
    slot = pl.program_id(0)
    scale = (1.0 - decay) / block

    def flat(value):
        return value.astype(f32).reshape(nz * piece, block).astype(bf16)

    def dot(a, b, over=((1,), (0,))):
        return lax.dot_general(a, b, (over, ((), ())), preferred_element_type=f32)

    for by, part in enumerate(g_parts):
        rows[:, lax.rem(y - by + ny, ny)] = part[:, slot].astype(f32)
    g = rows[...].reshape(block, block).astype(bf16)
    half = dot(flat(left_root[:, 0, slot]), g).astype(bf16)
    back[:, 2, 0] = dot(half, right_root[slot]).reshape(nz, piece, block).astype(bf16)
    left = dot(flat(g_parts[0][:, slot]), g, ((1,), (1,)))
    back[:, 0, 0] = (scale * left).reshape(nz, piece, block).astype(bf16)
    gram[...] = dot(g, g, ((0,), (0,))).reshape(gram.shape)
    back[:, 1, 0] = (scale * gram[:, y]).astype(bf16)


def products(g_parts, roots, right_root, y):
    ny = len(g_parts)
    nz, per, piece, block = g_parts[0].shape
    several = lambda n: pl.BlockSpec((nz, n, 1, piece, block), lambda s, _: (0, 0, s, 0, 0))
    return pl.pallas_call(
        products_kernel,
        grid_spec=pltpu.PrefetchScalarGridSpec(
            num_scalar_prefetch=1,
            grid=(per,),
            in_specs=[pl.BlockSpec(memory_space=pltpu.VMEM)] * (ny + 2),
            out_specs=several(3),
            scratch_shapes=[pltpu.VMEM((nz, ny, piece, block), f32)] * 2,
        ),
        out_shape=jax.ShapeDtypeStruct((nz, 3, per, piece, block), bf16),
        cost_estimate=pl.CostEstimate(
            flops=4 * per * block**3, bytes_accessed=24 * per * block * block, transcendentals=0
        ),
        compiler_params=params,
        name="products",
    )(y.astype(jnp.int32).reshape(1), *g_parts, roots, right_root)


def local(grad_parts, slot_table, left_stat, right_stat, left_root, right_root):
    nz, ny = lax.axis_size("z"), lax.axis_size("y")
    y = lax.axis_index("y")
    nblocks, piece, block = left_stat.shape[1:]
    rows_dev = grad_parts.shape[1]
    ncb = nblocks // (rows_dev // piece)
    per = nblocks // nz
    table = slot_table[0]
    by_owner = (nz, per, piece, block)

    def to_owner(value):
        return lax.all_to_all(value, "z", 0, 0, tiled=True)

    def from_y(value):
        far = [shift(value, "y", by) for by in (2, 1, 3)]
        return [value, far[1], far[0], far[2]]

    roots = to_owner(jnp.stack([left_root[0].reshape(by_owner), right_root[0].reshape(by_owner)], 1))
    placed = sum_dp(grad_parts[0], table, nblocks, piece, block)
    grads = to_owner(placed.reshape(by_owner))
    right = from_y(roots[:, 1])
    right = jnp.stack([lax.select_n((y - owner) % ny, *right) for owner in range(ny)])
    right = right.transpose(2, 1, 0, 3, 4).reshape(per, block, block)
    back = products(from_y(grads), roots, right, y)
    back, left_stat, right_stat = lax.optimization_barrier((back, left_stat, right_stat))
    back = lax.all_to_all(back, "z", 0, 0, tiled=True)
    left_stat, right_stat = (decay * left_stat.astype(f32), decay * right_stat.astype(f32))
    left_new, right_new, update = settle(
        table, back, left_stat[0], right_stat[0], rows_dev, ncb * block
    )
    return left_new[None], right_new[None], update


def solution(mesh):
    ny = 4
    devices = mesh.devices
    split = Mesh(
        devices.reshape(devices.shape[0] // 2, 2, devices.shape[1] // ny, ny), ("x", "core", "z", "y")
    )
    dp, fsdp = ("x", "core"), ("z", "y")
    factor = P(dp, None, fsdp, None)
    return jax.shard_map(
        local,
        mesh=split,
        in_specs=(P(dp, fsdp, None), P(dp, None), factor, factor, factor, factor),
        out_specs=(factor, factor, P(fsdp, dp)),
        check_vma=False,
    )
```

```python
import jax
import jax.numpy as jnp
from jax import lax
from jax.experimental import pallas as pl
from jax.experimental.pallas import tpu as pltpu
from jax.sharding import Mesh, PartitionSpec as P

decay = 0.9
bf16 = jnp.bfloat16
f32 = jnp.float32
params = pltpu.CompilerParams(vmem_limit_bytes=12 * 1024 * 1024)


def shift(value, axis, by):
    n = lax.axis_size(axis)
    return lax.ppermute(value, axis, [(i, (i + by) % n) for i in range(n)])


def add_kernel(where, grad, got, own, *refs):
    outs, (mine, theirs, sems) = refs[:-3], refs[-3:]
    count, _, band = mine.shape
    copies = []
    for i in range(count):
        columns = pl.ds(pl.multiple_of(where[i] * band, band), band)
        copies.append(
            (
                pltpu.make_async_copy(grad.at[:, columns], mine.at[i], sems.at[0, i]),
                pltpu.make_async_copy(got.at[:, columns], theirs.at[i], sems.at[1, i]),
            )
        )
        for copy in copies[i]:
            copy.start()
    for i in range(count):
        for copy in copies[i]:
            copy.wait()
        total = mine[i].astype(f32) + theirs[i].astype(f32)
        if i < len(outs):
            outs[i][...] = total.astype(bf16)
        else:
            own[...] = total


def total_kernel(table, own, first, second, third, out):
    nblocks, piece, block = out.shape
    ncb = own.shape[1] // block
    total = own[...] + first[...].astype(f32) + second[...].astype(f32) + third[...].astype(f32)
    for k in range(nblocks):
        row, col = k // ncb * piece, k % ncb * block
        out[table[k]] = total[row : row + piece, col : col + block].astype(bf16)


def spec(shape):
    return pl.BlockSpec(shape, lambda *_: (0,) * len(shape))


def sum_dp(grad, table, nblocks, piece, block):
    nx = lax.axis_size("x")
    core = lax.axis_index("core")
    x = lax.axis_index("x")
    rows, cols = grad.shape
    band = cols // (2 * nx)
    got = lax.ppermute(grad, "core", [(0, 1), (1, 0)])

    order = (2, 1, 3, 0)
    owners = jnp.stack([(x + by) % nx for by in order]).astype(jnp.int32)
    piece_spec = spec((rows, band))
    bf_piece = jax.ShapeDtypeStruct((rows, band), bf16)
    own, *pieces = pl.pallas_call(
        add_kernel,
        grid_spec=pltpu.PrefetchScalarGridSpec(
            num_scalar_prefetch=1,
            grid=(1,),
            in_specs=[pl.BlockSpec(memory_space=pltpu.HBM)] * 2,
            out_specs=[piece_spec] * nx,
            scratch_shapes=[pltpu.VMEM((nx, rows, band), bf16)] * 2 + [pltpu.SemaphoreType.DMA((2, nx))],
        ),
        out_shape=[jax.ShapeDtypeStruct((rows, band), f32)] + [bf_piece] * (nx - 1),
        cost_estimate=pl.CostEstimate(
            flops=rows * cols // 2, bytes_accessed=4 * rows * cols, transcendentals=0
        ),
        compiler_params=params,
        name="add_cores",
    )(2 * owners + core, grad, got)
    pieces = [shift(value, "x", by) for by, value in zip(order, pieces)]
    return pl.pallas_call(
        total_kernel,
        grid_spec=pltpu.PrefetchScalarGridSpec(
            num_scalar_prefetch=1,
            grid=(1,),
            in_specs=[piece_spec] * nx,
            out_specs=spec((nblocks, piece, block)),
        ),
        out_shape=jax.ShapeDtypeStruct((nblocks, piece, block), bf16),
        cost_estimate=pl.CostEstimate(
            flops=3 * rows * band, bytes_accessed=6 * rows * band * 2, transcendentals=0
        ),
        compiler_params=params,
        name="total_in_slots",
    )(table, own, *pieces)


def settle_kernel(table, back, left, right, left_new, right_new, update):
    nz, _, per, piece, block = back.shape
    ncb = update.shape[1] // block
    for arr, stat, new in ((0, left, left_new), (1, right, right_new)):
        gram = back[:, arr].astype(f32).reshape(nz * per, piece, block)
        new[...] = (stat[...] + gram).astype(bf16)
    for rb in range(0, update.shape[0] // piece, 2):
        for cb in range(ncb):
            pair = []
            for k in (rb * ncb + cb, (rb + 1) * ncb + cb):
                slot = table[k]
                pair.append(back[slot // per, 2, slot % per].astype(f32))
            update[rb * piece : (rb + 2) * piece, cb * block : (cb + 1) * block] = jnp.concatenate(
                pair, 0
            ).astype(bf16)


def settle(table, back, left, right, rows, cols):
    whole = lambda shape: pl.BlockSpec(shape, lambda i, t: (0,) * len(shape))
    return pl.pallas_call(
        settle_kernel,
        grid_spec=pltpu.PrefetchScalarGridSpec(
            num_scalar_prefetch=1,
            grid=(1,),
            in_specs=[pl.BlockSpec(memory_space=pltpu.VMEM)] * 3,
            out_specs=[whole(left.shape), whole(right.shape), whole((rows, cols))],
        ),
        out_shape=[
            jax.ShapeDtypeStruct(left.shape, bf16),
            jax.ShapeDtypeStruct(right.shape, bf16),
            jax.ShapeDtypeStruct((rows, cols), bf16),
        ],
        cost_estimate=pl.CostEstimate(
            flops=4 * left.size, bytes_accessed=8 * left.size * 2, transcendentals=0
        ),
        compiler_params=params,
        name="settle",
    )(table, back, left, right)


def products_kernel(where, *refs):
    g_parts, (left_root, right_root, back, rows, gram) = refs[:4], refs[4:]
    nz, _, _, piece, block = back.shape
    ny = len(g_parts)
    y = where[0]
    slot = pl.program_id(0)
    scale = (1.0 - decay) / block

    def flat(value):
        return value.astype(f32).reshape(nz * piece, block).astype(bf16)

    def dot(a, b, over=((1,), (0,))):
        return lax.dot_general(a, b, (over, ((), ())), preferred_element_type=f32)

    for by, part in enumerate(g_parts):
        rows[:, lax.rem(y - by + ny, ny)] = part[:, slot].astype(f32)
    g = rows[...].reshape(block, block).astype(bf16)
    half = dot(flat(left_root[:, 0, slot]), g).astype(bf16)
    back[:, 2, 0] = dot(half, right_root[slot]).reshape(nz, piece, block).astype(bf16)
    left = dot(flat(g_parts[0][:, slot]), g, ((1,), (1,)))
    back[:, 0, 0] = (scale * left).reshape(nz, piece, block).astype(bf16)
    gram[...] = dot(g, g, ((0,), (0,))).reshape(gram.shape)
    back[:, 1, 0] = (scale * gram[:, y]).astype(bf16)


def products(g_parts, roots, right_root, y):
    ny = len(g_parts)
    nz, per, piece, block = g_parts[0].shape
    several = lambda n: pl.BlockSpec((nz, n, 1, piece, block), lambda s, _: (0, 0, s, 0, 0))
    return pl.pallas_call(
        products_kernel,
        grid_spec=pltpu.PrefetchScalarGridSpec(
            num_scalar_prefetch=1,
            grid=(per,),
            in_specs=[pl.BlockSpec(memory_space=pltpu.VMEM)] * (ny + 2),
            out_specs=several(3),
            scratch_shapes=[pltpu.VMEM((nz, ny, piece, block), f32)] * 2,
        ),
        out_shape=jax.ShapeDtypeStruct((nz, 3, per, piece, block), bf16),
        cost_estimate=pl.CostEstimate(
            flops=4 * per * block**3, bytes_accessed=24 * per * block * block, transcendentals=0
        ),
        compiler_params=params,
        name="products",
    )(y.astype(jnp.int32).reshape(1), *g_parts, roots, right_root)


def local(grad_parts, slot_table, left_stat, right_stat, left_root, right_root):
    nz, ny = lax.axis_size("z"), lax.axis_size("y")
    y = lax.axis_index("y")
    nblocks, piece, block = left_stat.shape[1:]
    rows_dev = grad_parts.shape[1]
    ncb = nblocks // (rows_dev // piece)
    per = nblocks // nz
    table = slot_table[0]
    by_owner = (nz, per, piece, block)

    def to_owner(value):
        return lax.all_to_all(value, "z", 0, 0, tiled=True)

    def from_y(value):
        far = [shift(value, "y", by) for by in (2, 1, 3)]
        return [value, far[1], far[0], far[2]]

    roots = to_owner(jnp.stack([left_root[0].reshape(by_owner), right_root[0].reshape(by_owner)], 1))
    placed = sum_dp(grad_parts[0], table, nblocks, piece, block)
    grads = to_owner(placed.reshape(by_owner))
    right = from_y(roots[:, 1])
    right = jnp.stack([lax.select_n((y - owner) % ny, *right) for owner in range(ny)])
    right = right.transpose(2, 1, 0, 3, 4).reshape(per, block, block)
    back = products(from_y(grads), roots, right, y)
    back, left_stat, right_stat = lax.optimization_barrier((back, left_stat, right_stat))
    back = lax.all_to_all(back, "z", 0, 0, tiled=True)
    left_stat, right_stat = (decay * left_stat.astype(f32), decay * right_stat.astype(f32))
    left_new, right_new, update = settle(
        table, back, left_stat[0], right_stat[0], rows_dev, ncb * block
    )
    return left_new[None], right_new[None], update


def solution(mesh):
    ny = 4
    devices = mesh.devices
    split = Mesh(
        devices.reshape(devices.shape[0] // 2, 2, devices.shape[1] // ny, ny), ("x", "core", "z", "y")
    )
    dp, fsdp = ("x", "core"), ("z", "y")
    factor = P(dp, None, fsdp, None)
    return jax.shard_map(
        local,
        mesh=split,
        in_specs=(P(dp, fsdp, None), P(dp, None), factor, factor, factor, factor),
        out_specs=(factor, factor, P(fsdp, dp)),
        check_vma=False,
    )
```
